256 devices in a mesh: width: 8 (over z), hidden: 32 (over x, y, core).
Axes of the slice: x: 4, y: 4, z: 8, core: 2. Of those that a mesh axis runs over, the one named last changes fastest.
Arguments:
- tokens: bfloat16 [768, 16384], P('hidden', 'width'), may hold values from -6 to 6
- gate_weight: bfloat16 [16384, 28672], P('width', 'hidden'), may hold values from -0.046875 to 0.046875
- up_weight: bfloat16 [16384, 28672], P('width', 'hidden'), may hold values from -0.046875 to 0.046875
- down_weight: bfloat16 [28672, 16384], P('hidden', 'width'), may hold values from -0.03125 to 0.03125
Outputs:
- mixed: bfloat16 [768, 16384], P('hidden', 'width')
The draws below stay inside these ranges and needn't reach their ends.
All inputs are finite; a program needn't handle non-finite values.
Results may differ from the reference program's by a relative error of at most 0.0049.
Values may be sent and summed in bfloat16 or wider, within the bound.
No kernel may reach another device: no remote copies, remote signals or barrier semaphores. Data moves between devices by JAX's collectives and lax.ppermute only.
A program may use at most 64 MiB of HBM per device.

```python
import jax
import jax.numpy as jnp

D = 16384
FF = 28672
TOKENS = 768


def shard_levels(stream_key, dims, cuts, low, largest):
    loudness, own = 1.0, jax.random.fold_in(stream_key, 6)
    for dim, shards_of in cuts:
        heights = jnp.exp(jax.random.uniform(jax.random.fold_in(own, dim), (shards_of,), jnp.float32, low / len(cuts), largest / len(cuts)))
        loudness = loudness * jnp.repeat(heights, dims[dim] // shards_of).reshape([-1 if axis == dim else 1 for axis in range(len(dims))])
    return loudness


def centred(own_key, shape, width, reach, cuts=(), kind=jnp.bfloat16):
    level = shard_levels(own_key, shape, cuts, -0.22, 0.18) if cuts else 1.0
    drawn = jax.random.normal(own_key, shape, jnp.float32) * width * level
    return jnp.minimum(jnp.maximum(drawn, -reach), reach).astype(kind)


def setup_inputs(seed: int = 0) -> dict:
    keys = jax.random.split(jax.random.key(seed), 5)
    return {
        "tokens": centred(keys[0], (TOKENS, D), 1.0, 6.0, ((0, 32), (1, 8))),
        "gate_weight": centred(keys[1], (D, FF), D ** -0.5, 0.046875, ((0, 8), (1, 32))),
        "up_weight": centred(keys[2], (D, FF), D ** -0.5, 0.046875, ((0, 8), (1, 32))),
        "down_weight": centred(keys[3], (FF, D), FF ** -0.5, 0.03125, ((0, 32), (1, 8))),
    }


def reference(tokens, gate_weight, up_weight, down_weight):
    gate = jnp.dot(tokens, gate_weight, preferred_element_type=jnp.float32)
    up = jnp.dot(tokens, up_weight, preferred_element_type=jnp.float32)
    hidden = (jax.nn.silu(gate) * up).astype(jnp.bfloat16)
    mixed = jnp.dot(hidden, down_weight, preferred_element_type=jnp.float32)
    return mixed.astype(jnp.bfloat16)
```

```python
import jax
import jax.numpy as jnp
from jax import lax
from jax.sharding import PartitionSpec as P

W = "width"
H = "hidden"
NX = NY = 4
NZ = 8
BF = jnp.bfloat16
F16 = jnp.float16
F32 = jnp.float32


def place(x, y, c):
    return (x % NX * NY + y % NY) * 2 + c % 2


def moved(axis, d):
    pairs = []
    for x in range(NX):
        for y in range(NY):
            for c in range(2):
                along_x = (c == 0) == (axis == 0)
                to = place(x + d, y, c) if along_x else place(x, y + d, c)
                pairs.append((place(x, y, c), to))
    return pairs


SWAP = [(h, h ^ 1) for h in range(2 * NX * NY)]


def turn(d):
    return [(i, (i + d) % NZ) for i in range(NZ)]


def scale_of(tokens, gate_weight, up_weight):
    largest = jnp.stack(
        [
            jnp.max(jnp.abs(tokens)).astype(F32),
            jnp.maximum(jnp.max(jnp.abs(gate_weight)), jnp.max(jnp.abs(up_weight))).astype(F32),
        ]
    )
    largest = lax.pmax(largest, (H, W))
    bound = jnp.maximum(largest[0], 1e-12) * jnp.maximum(largest[1], 1e-12) * (NZ * gate_weight.shape[0])
    return 32768.0 / bound, bound * (1.0 / 32768.0)


def summed_over_width(part, z, scale):
    rows = part.shape[1] // 2

    def own(k, lo, hi):
        chunk = lax.dynamic_index_in_dim(part, lax.rem(z + k + NZ, NZ), 0, keepdims=False)
        return chunk[lo:hi] * scale

    full = part.shape[1]
    up = lax.ppermute(own(4, 0, rows).astype(F16), W, turn(1))
    down = lax.ppermute(own(-4, rows, full).astype(F16), W, turn(-1))
    for k in (3, 2, 1):
        if k == 3:
            send_up = jnp.concatenate([up.astype(F32) + own(3, 0, rows), own(3, rows, full)])
            send_down = jnp.concatenate([own(-3, 0, rows), down.astype(F32) + own(-3, rows, full)])
        else:
            send_up = up.astype(F32) + own(k, 0, full)
            send_down = down.astype(F32) + own(-k, 0, full)
        up = lax.ppermute(send_up.astype(F16), W, turn(1))
        down = lax.ppermute(send_down.astype(F16), W, turn(-1))
    return up.astype(F32) + down.astype(F32) + own(0, 0, full)


def gathered_over_width(own, z):
    rows = own.shape[0] // 2
    out = jnp.zeros((NZ,) + own.shape, own.dtype)

    def put(out, block, k):
        return lax.dynamic_update_slice(out, block[None], (lax.rem(z + k + NZ, NZ), 0, 0))

    out = put(out, own, 0)
    up = down = own
    for k in (1, 2, 3):
        up = lax.ppermute(up, W, turn(1))
        down = lax.ppermute(down, W, turn(-1))
        out = put(put(out, up, -k), down, k)
    far = jnp.concatenate(
        [lax.ppermute(up[:rows], W, turn(1)), lax.ppermute(down[rows:], W, turn(-1))]
    )
    return put(out, far, 4)


def shards(tokens, gate_weight, up_weight, down_weight):
    z = lax.axis_index(W)
    mine = tokens.shape[0]
    scale, unscale = scale_of(tokens, gate_weight, up_weight)

    line = jnp.concatenate([tokens] + [lax.ppermute(tokens, H, moved(0, -d)) for d in (1, 2, 3)])
    plane = jnp.concatenate([line] + [lax.ppermute(line, H, moved(1, -d)) for d in (1, 2, 3)])
    piece = jnp.concatenate([plane, lax.ppermute(plane, H, SWAP)])

    chunks = (NZ, piece.shape[0] // NZ, gate_weight.shape[1])
    gate_part = jnp.dot(piece, gate_weight, preferred_element_type=F32).reshape(chunks)
    up_part = jnp.dot(piece, up_weight, preferred_element_type=F32).reshape(chunks)
    gate = summed_over_width(gate_part, z, scale) * unscale
    up = summed_over_width(up_part, z, scale) * unscale
    hidden_units = gathered_over_width((jax.nn.silu(gate) * up).astype(BF), z)

    terms = jnp.dot(hidden_units.reshape(piece.shape[0], -1), down_weight, preferred_element_type=F32)
    half = terms.shape[0] // 2
    total = terms[:half] + lax.ppermute(terms[half:].astype(BF), H, SWAP).astype(F32)
    for axis in (1, 0):
        rows = total.shape[0] // 4
        sent = [lax.ppermute(total[d * rows : (d + 1) * rows].astype(BF), H, moved(axis, d)) for d in (1, 2, 3)]
        total = total[:rows] + sent[0].astype(F32) + sent[1].astype(F32) + sent[2].astype(F32)
    return total.astype(BF)


def solution(mesh):
    return jax.shard_map(
        shards,
        mesh=mesh,
        in_specs=(
            P(H, W),
            P(W, H),
            P(W, H),
            P(H, W),
        ),
        out_specs=P(H, W),
        check_vma=False,
    )
```

```python
import jax
import jax.numpy as jnp
from jax import lax
from jax.sharding import PartitionSpec as P

W = "width"
H = "hidden"
NX = NY = 4
NZ = 8
NH = 2 * NX * NY
BF = jnp.bfloat16
F16 = jnp.float16
F32 = jnp.float32


def place(x, y, c):
    return (x % NX * NY + y % NY) * 2 + c % 2


def further(h, axis, d):
    x, y, c = h // 2 // NY, h // 2 % NY, h % 2
    return place(x + d, y, c) if (c == 0) == (axis == 0) else place(x, y + d, c)


def along(axis, d):
    return [(h, further(h, axis, d)) for h in range(NH)]


SWAP = [(h, h ^ 1) for h in range(NH)]


def turn(d):
    return [(i, (i + d) % NZ) for i in range(NZ)]


def coded(v):
    root = lax.rsqrt(lax.rsqrt(jnp.maximum(jnp.abs(v) * 2.0**47, 1e-36)))
    return jnp.where(v < 0, -root, root).astype(F16)


def decoded(r):
    r = r.astype(F32)
    square = r * r
    return (r * jnp.abs(r)) * (square * 2.0**-47)


def summed_over_width(part, z):
    full = part.shape[1]
    half = full // 2

    def own(k, lo=0, hi=full):
        return lax.dynamic_index_in_dim(part, lax.rem(z + k + NZ, NZ), 0, keepdims=False)[lo:hi]

    up = lax.ppermute(coded(own(4, 0, half)), W, turn(1))
    down = lax.ppermute(coded(own(4, half)), W, turn(-1))
    for k in (3, 2, 1):
        if k == 3:
            a = jnp.concatenate([decoded(up) + own(3, 0, half), own(3, half)])
            b = jnp.concatenate([own(-3, 0, half), decoded(down) + own(-3, half)])
        else:
            a, b = decoded(up) + own(k), decoded(down) + own(-k)
        up = lax.ppermute(coded(a), W, turn(1))
        down = lax.ppermute(coded(b), W, turn(-1))
    return decoded(up) + decoded(down) + own(0)


def gathered_over_width(own, z):
    half = own.shape[0] // 2
    out = jnp.zeros((NZ,) + own.shape, own.dtype)

    def put(out, block, k):
        return lax.dynamic_update_slice(out, block[None], (lax.rem(z + k + NZ, NZ), 0, 0))

    out = put(out, own, 0)
    up = down = own
    for k in (1, 2, 3):
        up = lax.ppermute(up, W, turn(1))
        down = lax.ppermute(down, W, turn(-1))
        out = put(put(out, up, -k), down, k)
    far = jnp.concatenate(
        [lax.ppermute(up[:half], W, turn(1)), lax.ppermute(down[half:], W, turn(-1))]
    )
    return put(out, far, 4)


def dot(a, b):
    return jnp.dot(a, b, preferred_element_type=F32)


def shards(tokens, gate_weight, up_weight, down_weight):
    z = lax.axis_index(W)
    line = jnp.concatenate([tokens] + [lax.ppermute(tokens, H, along(0, -d)) for d in (1, 2, 3)])
    plane = jnp.concatenate([line] + [lax.ppermute(line, H, along(1, -d)) for d in (1, 2, 3)])
    other = lax.ppermute(plane, H, SWAP)

    def chunks(weight):
        both = jnp.concatenate([dot(plane, weight), dot(other, weight)])
        return both.reshape(NZ, -1, weight.shape[1])

    gate = summed_over_width(chunks(gate_weight), z)
    up = summed_over_width(chunks(up_weight), z)
    units = gathered_over_width((jax.nn.silu(gate) * up).astype(BF), z)

    half = NZ // 2
    wide = units.shape[2]
    theirs = dot(units[half:].reshape(-1, wide), down_weight).astype(BF)
    ours = dot(units[:half].reshape(-1, wide), down_weight)
    total = ours + lax.ppermute(theirs, H, SWAP).astype(F32)
    for axis in (1, 0):
        rows = total.shape[0] // 4
        sent = [
            lax.ppermute(total[d * rows : (d + 1) * rows].astype(BF), H, along(axis, d))
            for d in (1, 2, 3)
        ]
        total = total[:rows] + sent[0].astype(F32) + sent[1].astype(F32) + sent[2].astype(F32)
    return total.astype(BF)


def solution(mesh):
    return jax.shard_map(
        shards,
        mesh=mesh,
        in_specs=(
            P(H, W),
            P(W, H),
            P(W, H),
            P(H, W),
        ),
        out_specs=P(H, W),
        check_vma=False,
    )
```

```python
import jax
import jax.numpy as jnp
from jax import lax
from jax.sharding import PartitionSpec as P

W = "width"
H = "hidden"
NX = NY = 4
NZ = 8
NH = 2 * NX * NY
BF = jnp.bfloat16
F16 = jnp.float16
F32 = jnp.float32


def place(x, y, c):
    return (x % NX * NY + y % NY) * 2 + c % 2


def further(h, axis, d):
    x, y, c = h // 2 // NY, h // 2 % NY, h % 2
    return place(x + d, y, c) if (c == 0) == (axis == 0) else place(x, y + d, c)


def along(axis, d):
    return [(h, further(h, axis, d)) for h in range(NH)]


SWAP = [(h, h ^ 1) for h in range(NH)]


def turn(d):
    return [(i, (i + d) % NZ) for i in range(NZ)]


def coded(v):
    root = lax.rsqrt(lax.rsqrt(jnp.maximum(jnp.abs(v) * 2.0**47, 1e-36)))
    return jnp.where(v < 0, -root, root).astype(F16)


def decoded(r):
    r = r.astype(F32)
    square = r * r
    return (r * jnp.abs(r)) * (square * 2.0**-47)


def summed_over_width(part, z):
    full = part.shape[1]
    half = full // 2

    def own(k, lo=0, hi=full):
        return lax.dynamic_index_in_dim(part, lax.rem(z + k + NZ, NZ), 0, keepdims=False)[lo:hi]

    up = lax.ppermute(coded(own(4, 0, half)), W, turn(1))
    down = lax.ppermute(coded(own(4, half)), W, turn(-1))
    for k in (3, 2, 1):
        if k == 3:
            a = jnp.concatenate([decoded(up) + own(3, 0, half), own(3, half)])
            b = jnp.concatenate([own(-3, 0, half), decoded(down) + own(-3, half)])
        else:
            a, b = decoded(up) + own(k), decoded(down) + own(-k)
        up = lax.ppermute(coded(a), W, turn(1))
        down = lax.ppermute(coded(b), W, turn(-1))
    return decoded(up) + decoded(down) + own(0)


def gathered_over_width(own, z):
    out = jnp.zeros((NZ,) + own.shape, own.dtype)

    def put(out, block, k):
        return lax.dynamic_update_slice(out, block[None], (lax.rem(z + k + NZ, NZ), 0, 0))

    out = put(out, own, 0)
    up = down = own
    for k in (1, 2, 3):
        up = lax.ppermute(up, W, turn(1))
        down = lax.ppermute(down, W, turn(-1))
        out = put(put(out, up, -k), down, k)
    return put(out, lax.ppermute(up, W, turn(1)), 4)


def dot(a, b):
    return jnp.dot(a, b, preferred_element_type=F32)


def shards(tokens, gate_weight, up_weight, down_weight):
    z = lax.axis_index(W)
    line = jnp.concatenate([tokens] + [lax.ppermute(tokens, H, along(0, -d)) for d in (1, 2, 3)])
    plane = jnp.concatenate([line] + [lax.ppermute(line, H, along(1, -d)) for d in (1, 2, 3)])
    other = lax.ppermute(plane, H, SWAP)

    def chunks(weight):
        both = jnp.concatenate([dot(plane, weight), dot(other, weight)])
        return both.reshape(NZ, -1, weight.shape[1])

    gate = summed_over_width(chunks(gate_weight), z)
    up = summed_over_width(chunks(up_weight), z)
    units = gathered_over_width(lax.optimization_barrier((jax.nn.silu(gate) * up).astype(BF)), z)

    half = NZ // 2
    wide = units.shape[2]
    theirs = dot(units[half:].reshape(-1, wide), down_weight).astype(BF)
    ours = lax.optimization_barrier(dot(units[:half].reshape(-1, wide), down_weight))
    total = ours + lax.ppermute(theirs, H, SWAP).astype(F32)
    for axis in (1, 0):
        rows = total.shape[0] // 4
        sent = [
            lax.ppermute(total[d * rows : (d + 1) * rows].astype(BF), H, along(axis, d))
            for d in (1, 2, 3)
        ]
        total = total[:rows] + sent[0].astype(F32) + sent[1].astype(F32) + sent[2].astype(F32)
    return total.astype(BF)


def solution(mesh):
    return jax.shard_map(
        shards,
        mesh=mesh,
        in_specs=(
            P(H, W),
            P(W, H),
            P(W, H),
            P(H, W),
        ),
        out_specs=P(H, W),
        check_vma=False,
    )
```

```python
import jax
import jax.numpy as jnp
from jax import lax
from jax.sharding import PartitionSpec as P

W = "width"
H = "hidden"
NX = NY = 4
NZ = 8
NH = 2 * NX * NY
BF = jnp.bfloat16
F16 = jnp.float16
F32 = jnp.float32


def place(x, y, c):
    return (x % NX * NY + y % NY) * 2 + c % 2


def further(h, axis, d):
    x, y, c = h // 2 // NY, h // 2 % NY, h % 2
    return place(x + d, y, c) if (c == 0) == (axis == 0) else place(x, y + d, c)


def along(axis, d):
    return [(h, further(h, axis, d)) for h in range(NH)]


SWAP = [(h, h ^ 1) for h in range(NH)]


def turn(d):
    return [(i, (i + d) % NZ) for i in range(NZ)]


def coded(v):
    root = lax.rsqrt(lax.rsqrt(jnp.maximum(jnp.abs(v) * 2.0**47, 1e-36)))
    return jnp.where(v < 0, -root, root).astype(F16)


def decoded(r):
    r = r.astype(F32)
    square = r * r
    return (r * jnp.abs(r)) * (square * 2.0**-47)


def summed_over_width(part, z, far):
    def own(k):
        return lax.dynamic_index_in_dim(part, lax.rem(z + k + NZ, NZ), 0, keepdims=False)

    first = lax.ppermute(coded(own(4)), W, turn(far))
    up, down = (first, None) if far == 1 else (None, first)
    for k in (3, 2, 1):
        a = own(k) if up is None else decoded(up) + own(k)
        b = own(-k) if down is None else decoded(down) + own(-k)
        up = lax.ppermute(coded(a), W, turn(1))
        down = lax.ppermute(coded(b), W, turn(-1))
    return decoded(up) + decoded(down) + own(0)


def gathered_over_width(own, z):
    out = jnp.zeros((NZ,) + own.shape, own.dtype)

    def put(out, block, k):
        return lax.dynamic_update_slice(out, block[None], (lax.rem(z + k + NZ, NZ), 0, 0))

    out = put(out, own, 0)
    up = down = own
    for k in (1, 2, 3):
        up = lax.ppermute(up, W, turn(1))
        down = lax.ppermute(down, W, turn(-1))
        out = put(put(out, up, -k), down, k)
    return put(out, lax.ppermute(up, W, turn(1)), 4)


ORDER = (2, 1, 3)


def fetched(block, axis):
    got = {d: lax.ppermute(block, H, along(axis, -d)) for d in ORDER}
    return [got[d] for d in (1, 2, 3)]


def dot(a, b):
    return jnp.dot(a, b, preferred_element_type=F32)


def shards(tokens, gate_weight, up_weight, down_weight):
    z = lax.axis_index(W)
    line = jnp.concatenate([tokens] + fetched(tokens, 0))
    plane = jnp.concatenate([line] + fetched(line, 1))
    other = lax.ppermute(plane, H, SWAP)

    def chunks(weight):
        both = jnp.concatenate([dot(plane, weight), dot(other, weight)])
        return both.reshape(NZ, -1, weight.shape[1])

    gate = lax.optimization_barrier(jax.nn.silu(summed_over_width(chunks(gate_weight), z, 1)))
    up = summed_over_width(chunks(up_weight), z, -1)
    units = gathered_over_width(lax.optimization_barrier((gate * up).astype(BF)), z)

    half = NZ // 2
    wide = units.shape[2]
    theirs = dot(units[half:].reshape(-1, wide), down_weight).astype(BF)
    ours = lax.optimization_barrier(dot(units[:half].reshape(-1, wide), down_weight))
    total = ours + lax.ppermute(theirs, H, SWAP).astype(F32)
    for axis in (1, 0):
        rows = total.shape[0] // 4
        sent = [
            lax.ppermute(total[d * rows : (d + 1) * rows].astype(BF), H, along(axis, d))
            for d in ORDER
        ]
        total = total[:rows] + sent[0].astype(F32) + sent[1].astype(F32) + sent[2].astype(F32)
    return total.astype(BF)


def solution(mesh):
    return jax.shard_map(
        shards,
        mesh=mesh,
        in_specs=(
            P(H, W),
            P(W, H),
            P(W, H),
            P(H, W),
        ),
        out_specs=P(H, W),
        check_vma=False,
    )
```

```python
import jax
import jax.numpy as jnp
from jax import lax
from jax.sharding import PartitionSpec as P

W = "width"
H = "hidden"
NX = NY = 4
NZ = 8
NH = 2 * NX * NY
BF = jnp.bfloat16
F16 = jnp.float16
F32 = jnp.float32


def place(x, y, c):
    return (x % NX * NY + y % NY) * 2 + c % 2


def further(h, axis, d):
    x, y, c = h // 2 // NY, h // 2 % NY, h % 2
    return place(x + d, y, c) if (c == 0) == (axis == 0) else place(x, y + d, c)


def along(axis, d):
    return [(h, further(h, axis, d)) for h in range(NH)]


SWAP = [(h, h ^ 1) for h in range(NH)]


def turn(d):
    return [(i, (i + d) % NZ) for i in range(NZ)]


def coded(v):
    root = lax.rsqrt(lax.rsqrt(jnp.maximum(jnp.abs(v) * 2.0**47, 1e-36)))
    return jnp.where(v < 0, -root, root).astype(F16)


def decoded(r):
    r = r.astype(F32)
    square = r * r
    return (r * jnp.abs(r)) * (square * 2.0**-47)


def summed_over_width(part, z, far):
    def own(k):
        return lax.dynamic_index_in_dim(part, lax.rem(z + k + NZ, NZ), 0, keepdims=False)

    first = lax.ppermute(coded(own(4)), W, turn(far))
    up, down = (first, None) if far == 1 else (None, first)
    for k in (3, 2, 1):
        a = own(k) if up is None else decoded(up) + own(k)
        b = own(-k) if down is None else decoded(down) + own(-k)
        up = lax.ppermute(coded(a), W, turn(1))
        down = lax.ppermute(coded(b), W, turn(-1))
    return decoded(up) + decoded(down) + own(0)


def gathered_over_width(own, z):
    out = jnp.zeros((NZ,) + own.shape, own.dtype)

    def put(out, block, k):
        return lax.dynamic_update_slice(out, block[None], (lax.rem(z + k + NZ, NZ), 0, 0))

    out = put(out, own, 0)
    up = down = own
    for k in (1, 2, 3):
        up = lax.ppermute(up, W, turn(1))
        down = lax.ppermute(down, W, turn(-1))
        out = put(put(out, up, -k), down, k)
    return put(out, lax.ppermute(up, W, turn(1)), 4)


ORDER = (2, 1, 3)


def fetched(block, axis):
    got = {d: lax.ppermute(block, H, along(axis, -d)) for d in ORDER}
    return [got[d] for d in (1, 2, 3)]


def dot(a, b):
    return jnp.dot(a, b, preferred_element_type=F32)


def shards(tokens, gate_weight, up_weight, down_weight):
    z = lax.axis_index(W)
    line = jnp.concatenate([tokens] + fetched(tokens, 0))
    plane = jnp.concatenate([line] + fetched(line, 1))
    other = lax.ppermute(plane, H, SWAP)

    def chunks(weight):
        both = jnp.concatenate([dot(plane, weight), dot(other, weight)])
        return both.reshape(NZ, -1, weight.shape[1])

    gate = jax.nn.silu(summed_over_width(chunks(gate_weight), z, 1))
    up = summed_over_width(chunks(up_weight), z, -1)
    units = gathered_over_width(lax.optimization_barrier((gate * up).astype(BF)), z)

    half = NZ // 2
    wide = units.shape[2]
    theirs = dot(units[half:].reshape(-1, wide), down_weight).astype(BF)
    ours = lax.optimization_barrier(dot(units[:half].reshape(-1, wide), down_weight))
    total = ours + lax.ppermute(theirs, H, SWAP).astype(F32)
    for axis in (1, 0):
        rows = total.shape[0] // 4
        sent = [
            lax.ppermute(total[d * rows : (d + 1) * rows].astype(BF), H, along(axis, d))
            for d in ORDER
        ]
        total = total[:rows] + sent[0].astype(F32) + sent[1].astype(F32) + sent[2].astype(F32)
    return total.astype(BF)


def solution(mesh):
    return jax.shard_map(
        shards,
        mesh=mesh,
        in_specs=(
            P(H, W),
            P(W, H),
            P(W, H),
            P(H, W),
        ),
        out_specs=P(H, W),
        check_vma=False,
    )
```

```python
import jax
import jax.numpy as jnp
from jax import lax
from jax.sharding import PartitionSpec as P

W = "width"
H = "hidden"
NX = NY = 4
NZ = 8
NH = 2 * NX * NY
BF = jnp.bfloat16
F16 = jnp.float16
F32 = jnp.float32


def place(x, y, c):
    return (x % NX * NY + y % NY) * 2 + c % 2


def further(h, axis, d):
    x, y, c = h // 2 // NY, h // 2 % NY, h % 2
    return place(x + d, y, c) if (c == 0) == (axis == 0) else place(x, y + d, c)


def along(axis, d):
    return [(h, further(h, axis, d)) for h in range(NH)]


SWAP = [(h, h ^ 1) for h in range(NH)]


def turn(d):
    return [(i, (i + d) % NZ) for i in range(NZ)]


def coded(v):
    root = lax.rsqrt(lax.rsqrt(jnp.maximum(jnp.abs(v) * 2.0**47, 1e-36)))
    return jnp.where(v < 0, -root, root).astype(F16)


def decoded(r):
    r = r.astype(F32)
    square = r * r
    return (r * jnp.abs(r)) * (square * 2.0**-47)


def summed_over_width(part, z, far):
    def own(k):
        return lax.dynamic_index_in_dim(part, lax.rem(z + k + NZ, NZ), 0, keepdims=False)

    first = lax.ppermute(coded(own(4)), W, turn(far))
    up, down = (first, None) if far == 1 else (None, first)
    for k in (3, 2, 1):
        a = own(k) if up is None else decoded(up) + own(k)
        b = own(-k) if down is None else decoded(down) + own(-k)
        up = lax.ppermute(coded(a), W, turn(1))
        down = lax.ppermute(coded(b), W, turn(-1))
    return decoded(up) + decoded(down) + own(0)


def gathered_over_width(own, z):
    out = jnp.zeros((NZ,) + own.shape, own.dtype)

    def put(out, block, k):
        return lax.dynamic_update_slice(out, block[None], (lax.rem(z + k + NZ, NZ), 0, 0))

    out = put(out, own, 0)
    up = down = own
    for k in (1, 2, 3):
        up = lax.ppermute(up, W, turn(1))
        down = lax.ppermute(down, W, turn(-1))
        out = put(put(out, up, -k), down, k)
    return put(out, lax.ppermute(up, W, turn(1)), 4)


ORDER = (2, 1, 3)


def fetched(block, axis):
    got = {d: lax.ppermute(block, H, along(axis, -d)) for d in ORDER}
    return [got[d] for d in (1, 2, 3)]


def dot(a, b):
    return jnp.dot(a, b, preferred_element_type=F32)


def shards(tokens, gate_weight, up_weight, down_weight):
    z = lax.axis_index(W)
    line = jnp.concatenate([tokens] + fetched(tokens, 0))
    plane = jnp.concatenate([line] + fetched(line, 1))
    other = lax.ppermute(plane, H, SWAP)

    def chunks(weight):
        both = jnp.concatenate([dot(plane, weight), dot(other, weight)])
        return both.reshape(NZ, -1, weight.shape[1])

    gate = jax.nn.silu(summed_over_width(chunks(gate_weight), z, 1))
    up = summed_over_width(chunks(up_weight), z, -1)
    units = gathered_over_width(lax.optimization_barrier((gate * up).astype(BF)), z)

    half = NZ // 2
    wide = units.shape[2]
    theirs = dot(units[half:].reshape(-1, wide), down_weight).astype(BF)
    ours = lax.optimization_barrier(dot(units[:half].reshape(-1, wide), down_weight))
    theirs = lax.ppermute(theirs, H, SWAP)
    rows = ours.shape[0] // 4
    lines = [slice(d * rows, (d + 1) * rows) for d in range(4)]
    total = [ours[at] + theirs[at].astype(F32) for at in lines]
    for axis in (1, 0):
        sent = {}
        for d in ORDER:
            ready = total[d].astype(BF)
            if d == ORDER[0]:
                ready = lax.optimization_barrier(ready)
            sent[d] = lax.ppermute(ready, H, along(axis, d)).astype(F32)
        total = total[0] + sent[1] + sent[2] + sent[3]
        if axis == 1:
            total = jnp.split(total, 4)
    return total.astype(BF)


def solution(mesh):
    return jax.shard_map(
        shards,
        mesh=mesh,
        in_specs=(
            P(H, W),
            P(W, H),
            P(W, H),
            P(H, W),
        ),
        out_specs=P(H, W),
        check_vma=False,
    )
```
